32 devices in a mesh: row: 8 (over z, y), col: 4 (over x, core).
Axes of the slice: x: 2, y: 2, z: 4, core: 2. Of those that a mesh axis runs over, the one named last changes fastest.
Arguments:
- design: bfloat16 [5120, 8192], P('row', 'col'), may hold values from -0.125 to 0.125
- projector: bfloat16 [4, 5120, 640], P('col', 'row')
- targets: float32 [5120], P('row'), may hold values from -6 to 6
- sparsity: float32 [32], replicated, may hold values from 0.02 to 0.6
- ridge_weight: float32 [32], replicated, may hold values from 0.05 to 2
- coefficients: float32 [32, 8192], P(None, 'col'), may hold values from -4 to 4
- block_duals: float32 [8, 32, 8192], P('row', None, 'col'), may hold values from -4 to 4
- row_duals: float32 [32, 5120], P(None, 'row'), may hold values from -3 to 3
- block_fits: float32 [4, 32, 5120], P('col', None, 'row'), may hold values from -3 to 3
Outputs:
- estimate: float32 [32, 8192], P(None, 'col')
- column_duals: float32 [32, 8192], P(None, 'col')
- next_block_duals: float32 [8, 32, 8192], P('row', None, 'col')
- next_row_duals: float32 [32, 5120], P(None, 'row')
The draws below stay inside these ranges and needn't reach their ends.
All inputs are finite; a program needn't handle non-finite values.
Results may differ from the reference program's by a relative error of at most 0.013.
Values sent between devices are 32-bit elements; how exact they have to be, the bound alone decides.
A program may use at most 64 MiB of HBM per device.

```python
import math
import jax
import jax.numpy as jnp
from jax import lax

MR = 640
NC = 2048
L = 32
ITERS = 5
M = 5120
N = 8192
N_ROW = 8
N_COL = 4


def draw_projector(key, part):
    key = jax.random.fold_in(key, 7)
    noise_key, diag_key = jax.random.split(key)
    col_blocks = N // NC
    row_blocks = M // MR
    block_shape = (col_blocks, row_blocks, MR, MR)
    noise_part = jax.random.normal(noise_key, block_shape, jnp.float32) * (0.3 / math.sqrt(MR))
    diagonal = jnp.exp(jax.random.uniform(diag_key, block_shape[:3], jnp.float32, math.log(0.3), math.log(0.7)))
    noise_part = noise_part + jnp.swapaxes(noise_part, 2, 3)
    identity = (lax.broadcasted_iota(jnp.int32, (MR, MR), 0) == lax.broadcasted_iota(jnp.int32, (MR, MR), 1)).astype(jnp.float32)
    matrix = noise_part * (1.0 - identity) + diagonal[..., None] * identity
    return matrix.reshape(col_blocks, M, MR).astype(jnp.bfloat16)


def with_spikes(values, rng, source, target, shards_of, factor):
    def block_of(axis_at):
        return (jnp.arange(values.shape[axis_at]) // (values.shape[axis_at] // shards_of)).reshape((-1,) + (1,) * (values.ndim - 1 - axis_at))

    near = jax.random.permutation(rng, shards_of)[block_of(target)]
    far = (block_of(target) + shards_of // 2) % shards_of
    return jnp.where((block_of(source) == near) | (block_of(source) == far), factor * values, values)


def shard_levels(stream_key, extent, cuts, low, top_value):
    gain = 1.0
    for axis_at, parts in cuts:
        heights = jax.random.uniform(jax.random.fold_in(jax.random.fold_in(stream_key, 6), axis_at), (parts,), jnp.float32, low / len(cuts), top_value / len(cuts))
        gain = gain * jnp.repeat(jnp.exp(heights), extent[axis_at] // parts).reshape((-1,) + (1,) * (len(extent) - 1 - axis_at))
    return gain


def normal_values(key, dims, spread, limit, pieces=(), dtype=jnp.bfloat16):
    result = spread * jax.random.normal(key, dims, jnp.float32)
    if pieces:
        result = result * shard_levels(key, dims, pieces, -0.22, 0.18)
    return jnp.clip(result, -limit, limit).astype(dtype)


def heavy_noise(rng, shape, scale, limit, shards, heavy, held_as=jnp.bfloat16):
    drawn = scale * jax.random.normal(rng, shape, jnp.float32)
    if shards:
        drawn = drawn * shard_levels(rng, shape, shards, -0.22, 0.18)
    return jnp.clip(with_spikes(drawn, jax.random.fold_in(rng, 3), *heavy), -limit, limit).astype(held_as)


def setup_inputs(seed: int = 0) -> dict:
    splits = jax.random.split(jax.random.key(seed), 10)
    return {
        "design": normal_values(splits[0], (M, N), NC ** -0.5, 0.125, ((0, 8), (1, 4))),
        "projector": draw_projector(jax.random.fold_in(splits[9], 71), 0),
        "targets": normal_values(splits[2], (M,), 1.0, 6.0, ((0, 8),), jnp.float32),
        "sparsity": jnp.clip(jnp.exp(jax.random.uniform(splits[3], (L,), jnp.float32, math.log(0.02), math.log(0.6))), 0.02, 0.6),
        "ridge_weight": jnp.clip(jnp.exp(jax.random.uniform(splits[4], (L,), jnp.float32, math.log(0.05), math.log(2.0))), 0.05, 2.0),
        "coefficients": normal_values(splits[5], (L, N), 0.5, 4.0, ((1, 4),), jnp.float32),
        "block_duals": heavy_noise(splits[6], (N_ROW, L, N), 0.5, 4.0, ((0, 8), (2, 4)), (0, 2, 8, 2.0), jnp.float32),
        "row_duals": normal_values(splits[7], (L, M), 0.3, 3.0, ((1, 8),), jnp.float32),
        "block_fits": normal_values(splits[8], (N_COL, L, M), 0.3, 3.0, ((0, 4), (2, 8)), jnp.float32),
    }


def shrink(values, threshold):
    return jnp.maximum(values - threshold, 0.0) - jnp.maximum(-values - threshold, 0.0)


def rounded(values):
    narrow = lax.optimization_barrier(values.astype(jnp.bfloat16))
    return narrow.astype(jnp.float32)


def reference(design, projector, targets, sparsity, ridge_weight, coefficients, block_duals, row_duals, block_fits):
    matrix = design.astype(jnp.float32).reshape(N_ROW, MR, N_COL, NC)
    inverse = projector.astype(jnp.float32).reshape(N_COL, N_ROW, MR, MR)
    shares = block_duals.reshape(N_ROW, L, N_COL, NC)
    current = coefficients.reshape(L, N_COL, NC)
    fits = block_fits.reshape(N_COL, L, N_ROW, MR)
    duals_row = row_duals.reshape(L, N_ROW, MR)
    goals = targets.reshape(N_ROW, MR)
    threshold = sparsity[:, None, None]
    shrink_by = 1.0 / (1.0 + ridge_weight[:, None, None])
    column_dual = -jnp.sum(shares, axis=0)
    row_fit = jnp.sum(fits, axis=0)
    for iteration in range(ITERS):
        half_row = 0.5 * (row_fit - duals_row + goals[None])
        half_col = shrink(current - column_dual, threshold) * shrink_by
        lifted = fits + duals_row[None]
        start = current[None] - shares + jnp.einsum('jlia,iajn->iljn', rounded(lifted), matrix)
        image = jnp.einsum('iljn,iajn->jlia', rounded(start), matrix)
        weighted = jnp.einsum('jlia,jiab->jlib', rounded(image), inverse)
        block_x = start - jnp.einsum('jlib,ibjn->iljn', rounded(weighted), matrix)
        block_y = jnp.einsum('iljn,iajn->jlia', rounded(block_x), matrix)
        average = (half_col + jnp.sum(block_x, axis=0)) / (N_ROW + 1)
        column_dual = column_dual + half_col - average
        shares = shares + block_x - average[None]
        misfit = (half_row - jnp.sum(block_y, axis=0)) / (N_COL + 1)
        row_fit = half_row - misfit
        fits = block_y + misfit[None]
        duals_row = duals_row + misfit
        current = average
    return (current.reshape(L, N), column_dual.reshape(L, N),
            shares.reshape(N_ROW, L, N), duals_row.reshape(L, M))
```

```python
import functools

import jax
import jax.numpy as jnp
from jax import lax
from jax.experimental import pallas as pl
from jax.experimental.pallas import tpu as pltpu
from jax.sharding import PartitionSpec as P

ITERS = 5
MESH = pl.DeviceIdType.MESH
BF16 = jnp.bfloat16
F32 = jnp.float32


def shrink(values, threshold):
    return jnp.maximum(values - threshold, 0.0) - jnp.maximum(-values - threshold, 0.0)


def times(left, right):
    return jnp.dot(left, right, preferred_element_type=F32)


def times_transpose(left, right):
    return lax.dot_general(left, right, (((1,), (1,)), ((), ())), preferred_element_type=F32)


def kernel(
    rows, cols, split,
    design, projector, targets, sparsity, ridge, coefficients, block_duals, row_duals, block_fits,
    o_z, o_xc, o_xd, o_yd,
    A, K, S, XD, PX, AV, XB, PY, FIT, YD, YR, U, THR, SHR, XC, HC,
    R1, T1, R2, Q1, G1, Q2,
    load_a, load_k, load_v, load_x, load_z, store,
    s1_send, s1_recv, s2_send, s2_recv, q1_send, q1_recv, q2_send, q2_recv,
    z_send, z_recv, y_send, y_recv, bz_send, bz_recv, by_send, by_recv, p_send, p_recv,
):
    depth = rows // 2
    blocks, size, width = S.shape
    part = size // split
    me_row, me_col = lax.axis_index("row"), lax.axis_index("col")
    hi, lo = me_row // 2, me_row % 2
    pair = {"row": 2 * hi + 1 - lo}

    def near(k):
        return lax.rem(hi + k + depth, depth)

    def line(k):
        return {"row": 2 * near(k) + lo}

    def beside(k):
        return {"col": lax.rem(me_col + k, cols)}

    def block_of(p):
        return p // split

    def piece(ref, p):
        if split == 1:
            return ref.at[p]
        return ref.at[p // split, pl.ds(pl.multiple_of((p % split) * part, part), part), :]

    def remote(src, dst, send, recv, device):
        return pltpu.make_async_remote_copy(
            src_ref=src, dst_ref=dst, send_sem=send, recv_sem=recv, device_id=device, device_id_type=MESH)

    def columns(c):
        return pl.ds(c * width, width)

    order = list(range(1, depth)) + [0]

    barrier = pltpu.get_barrier_semaphore()
    peers = [pair] + [line(k) for k in range(1, depth)] + [beside(k) for k in range(1, cols)]
    for peer in peers:
        pl.semaphore_signal(barrier, inc=1, device_id=peer, device_id_type=MESH)

    load_xd = [pltpu.make_async_copy(block_duals.at[0, :, columns(c)], XD.at[c], load_x.at[c]) for c in range(blocks)]
    load_fit = pltpu.make_async_copy(block_fits.at[0], FIT, load_v.at[0])
    load_yd = pltpu.make_async_copy(row_duals, YD, load_v.at[1])
    load_zs = [pltpu.make_async_copy(coefficients.at[:, columns(c)], AV.at[c], load_z.at[c]) for c in range(blocks)]
    load_as = [pltpu.make_async_copy(design.at[:, columns(c)], A.at[c], load_a.at[c]) for c in range(blocks)]
    load_kk = pltpu.make_async_copy(projector.at[0], K, load_k.at[0])
    for copy in load_xd + [load_fit, load_yd]:
        copy.start()
    for c in range(blocks):
        load_as[c].start()
        load_zs[c].start()
    load_kk.start()

    eye = lax.broadcasted_iota(jnp.int32, (size, size), 0) == lax.broadcasted_iota(jnp.int32, (size, size), 1)

    def upright(ref):
        return jnp.sum(jnp.where(eye, ref[...], 0.0), axis=1, keepdims=True)

    THR[...] = jnp.broadcast_to(upright(sparsity), (size, width))
    SHR[...] = jnp.broadcast_to(1.0 / (1.0 + upright(ridge)), (size, width))

    pl.semaphore_wait(barrier, len(peers))

    for copy in load_xd:
        copy.wait()
    first = {}
    for k in order:
        first[k] = remote(piece(XD, 2 * near(k) + 1 - lo), Q1.at[k], q1_send.at[k], q1_recv.at[k], pair)
        first[k].start()
    load_fit.wait()
    load_yd.wait()

    def send_fit(slot, k):
        return remote(PY.at[slot, me_col], PY.at[slot, me_col], p_send.at[slot, k - 1], p_recv.at[slot, k - 1], beside(k))

    def take_fit(slot, k):
        source = lax.rem(me_col + cols - k, cols)
        remote(PY.at[slot, source], PY.at[slot, source], p_send.at[slot, k - 1], p_recv.at[slot, k - 1], beside(k)).wait_recv()

    def sum_fit(slot):
        total = PY[slot, 0]
        for j in range(1, cols):
            total = total + PY[slot, j]
        return total

    PY[2, me_col] = FIT[...]
    for k in range(1, cols):
        send_fit(2, k).start()

    lifted = (FIT[...] + YD[...]).astype(BF16)
    total_u = None
    for c in range(blocks):
        load_as[c].wait()
        load_zs[c].wait()
        s = AV[c] - XD[c] + times(lifted, A[c])
        S[c] = s
        u = times_transpose(s.astype(BF16), A[c])
        total_u = u if total_u is None else total_u + u
    U[...] = total_u

    for k in order:
        first[k].wait_recv()
        G1[k] = piece(XD, 2 * near(k) + lo)[...] + Q1[k]
        if k:
            remote(G1.at[k], Q2.at[k - 1], q2_send.at[k - 1], q2_recv.at[k - 1], line(k)).start()
    load_kk.wait()

    def stage_one(k):
        return remote(piece(PX, 2 * near(k) + 1 - lo), R1.at[k], s1_send.at[k], s1_recv.at[k], pair)

    def stage_two(k):
        return remote(T1.at[k], R2.at[k - 1], s2_send.at[k - 1], s2_recv.at[k - 1], line(k))

    def spread_line(ref, send, recv, k):
        mine = piece(ref, me_row)
        return remote(mine, mine, send.at[k - 1], recv.at[k - 1], line(k))

    def take_line(ref, send, recv, k):
        other = piece(ref, 2 * near(-k) + lo)
        remote(other, other, send.at[k - 1], recv.at[k - 1], line(k)).wait_recv()

    def spread_pair(ref, send, recv, k):
        other = piece(ref, 2 * near(-k) + lo)
        return remote(other, other, send.at[k], recv.at[k], pair)

    def take_pair(ref, send, recv, k):
        other = piece(ref, 2 * near(-k) + 1 - lo)
        remote(other, other, send.at[k], recv.at[k], pair).wait_recv()

    def project(slot):
        w = times(U[...].astype(BF16), K[...]).astype(BF16)

        def block_x(c):
            PX[c] = S[c] - times(w, A[c])

        for k in order:
            block_x(block_of(2 * near(k) + 1 - lo))
            stage_one(k).start()
        if split == 1:
            for k in order:
                block_x(2 * near(k) + lo)
        block_y = None
        for c in range(blocks):
            y = times_transpose(PX[c].astype(BF16), A[c])
            block_y = y if block_y is None else block_y + y
        PY[slot, me_col] = block_y
        for k in range(1, cols):
            send_fit(slot, k).start()
        for k in order:
            stage_one(k).wait_recv()
            T1[k] = piece(PX, 2 * near(k) + lo)[...] + R1[k]
            if k:
                stage_two(k).start()

    my_rows = pl.ds(pl.multiple_of((me_row % split) * part, part), part)

    def half_col():
        return shrink(piece(AV, me_row)[...] - XC[...], THR[my_rows, :]) * SHR[my_rows, :]

    def average():
        total = T1[0]
        for k in range(1, depth):
            stage_two(k).wait_recv()
            total = total + R2[k - 1]
        avg = (HC[...] + total) / (rows + 1)
        piece(AV, me_row)[...] = avg
        for k in range(1, depth):
            spread_line(AV, z_send, z_recv, k).start()
        spread_pair(AV, y_send, y_recv, 0).start()
        return avg

    def row_update(slot):
        half_row = 0.5 * (YR[...] - YD[...] + targets[...])
        for k in range(1, cols):
            take_fit(slot, k)
        misfit = (half_row - sum_fit(slot)) / (cols + 1)
        YR[...] = half_row - misfit
        YD[...] = YD[...] + misfit
        return misfit

    def settle(slot):
        for k in order:
            stage_one(k).wait_send()
            if k:
                stage_two(k).wait_send()
                spread_line(AV, z_send, z_recv, k).wait_send()
            spread_pair(AV, y_send, y_recv, k).wait_send()
        for k in range(1, cols):
            send_fit(slot, k).wait_send()

    def relay(ref, send, recv, pair_send, pair_recv):
        for k in range(1, depth):
            take_line(ref, send, recv, k)
            spread_pair(ref, pair_send, pair_recv, k).start()

    project(0)

    total = G1[0]
    for k in range(1, depth):
        remote(G1.at[k], Q2.at[k - 1], q2_send.at[k - 1], q2_recv.at[k - 1], line(k)).wait_recv()
        total = total + Q2[k - 1]
    XC[...] = -total
    HC[...] = half_col()
    for k in range(1, cols):
        take_fit(2, k)
    YR[...] = sum_fit(2)
    for k in range(1, cols):
        send_fit(2, k).wait_send()
    for k in order:
        first[k].wait_send()
        if k:
            remote(G1.at[k], Q2.at[k - 1], q2_send.at[k - 1], q2_recv.at[k - 1], line(k)).wait_send()

    def step(t, carry):
        slot = lax.rem(t, 2)
        avg = average()
        XC[...] = XC[...] + HC[...] - avg
        HC[...] = half_col()
        misfit = row_update(slot)
        lifted = (PY[slot, me_col] + misfit + YD[...]).astype(BF16)
        for c in range(blocks):
            S[c] = times(lifted, A[c])

        def arrived(p):
            c = block_of(p)
            duals = XD[c] + PX[c] - AV[c]
            XD[c] = duals
            s = AV[c] - duals + S[c]
            S[c] = s
            return times_transpose(s.astype(BF16), A[c])

        relay(AV, z_send, z_recv, y_send, y_recv)
        total_u = jnp.zeros(U.shape, F32)
        if split == 1:
            for k in range(depth):
                total_u = total_u + arrived(2 * near(-k) + lo)
        for k in range(depth):
            take_pair(AV, y_send, y_recv, k)
            total_u = total_u + arrived(2 * near(-k) + 1 - lo)
        U[...] = total_u
        settle(slot)
        project(1 - slot)
        return carry

    lax.fori_loop(0, ITERS - 1, step, 0)

    slot = (ITERS - 1) % 2
    piece(XB, me_row)[...] = XC[...] + HC[...]
    for k in range(1, depth):
        spread_line(XB, bz_send, bz_recv, k).start()
    spread_pair(XB, by_send, by_recv, 0).start()
    average()
    relay(XB, bz_send, bz_recv, by_send, by_recv)
    row_update(slot)
    stores = [pltpu.make_async_copy(YD, o_yd, store.at[0, 0])]
    stores[0].start()
    relay(AV, z_send, z_recv, y_send, y_recv)

    def finish(p):
        c = block_of(p)
        where = pl.ds(pl.multiple_of(c * width, width), width)
        XD[c] = XD[c] + PX[c] - AV[c]
        XB[c] = XB[c] - AV[c]
        n = len(stores)
        for ref, out in ((AV, o_z), (XB, o_xc), (XD, o_xd.at[0])):
            copy = pltpu.make_async_copy(ref.at[c], out.at[:, where], store.at[n, len(stores) - n])
            copy.start()
            stores.append(copy)

    for k in range(depth):
        spread_pair(XB, by_send, by_recv, k).wait_send()
        if k:
            spread_line(XB, bz_send, bz_recv, k).wait_send()
    if split == 1:
        for k in range(depth):
            finish(2 * near(-k) + lo)
    for k in range(depth):
        take_pair(XB, by_send, by_recv, k)
        take_pair(AV, y_send, y_recv, k)
        finish(2 * near(-k) + 1 - lo)
    settle(slot)
    for copy in stores:
        copy.wait()


def per_device(design, projector, targets, sparsity, ridge_weight, coefficients, block_duals, row_duals, block_fits):
    rows, cols = lax.axis_size("row"), lax.axis_size("col")
    size, n = coefficients.shape
    m = design.shape[0]
    width = max(128, n // rows)
    blocks = n // width
    split = rows // blocks
    part, depth = size // split, rows // 2
    any_space = pl.BlockSpec(memory_space=pl.ANY)
    vmem = pl.BlockSpec(memory_space=pltpu.VMEM)
    dma = pltpu.SemaphoreType.DMA
    wide = pltpu.VMEM((blocks, size, width), F32)
    tall = pltpu.VMEM((size, m), F32)
    own = pltpu.VMEM((part, width), F32)

    def pieces(count):
        return pltpu.VMEM((count, part, width), F32)

    scratch = [
        pltpu.VMEM((blocks, m, width), BF16), pltpu.VMEM((m, m), BF16),
        wide, wide, wide, wide, wide,
        pltpu.VMEM((3, cols, size, m), F32), tall, tall, tall, tall,
        pltpu.VMEM((size, width), F32), pltpu.VMEM((size, width), F32), own, own,
        pieces(depth), pieces(depth), pieces(depth - 1), pieces(depth), pieces(depth), pieces(depth - 1),
        dma((blocks,)), dma((1,)), dma((2,)), dma((blocks,)), dma((blocks,)), dma((3 * blocks + 1, 3)),
        dma((depth,)), dma((depth,)), dma((depth - 1,)), dma((depth - 1,)),
        dma((depth,)), dma((depth,)), dma((depth - 1,)), dma((depth - 1,)),
        dma((depth - 1,)), dma((depth - 1,)), dma((depth,)), dma((depth,)),
        dma((depth - 1,)), dma((depth - 1,)), dma((depth,)), dma((depth,)),
        dma((3, cols - 1)), dma((3, cols - 1)),
    ]
    return pl.pallas_call(
        functools.partial(kernel, rows, cols, split),
        out_shape=(
            jax.ShapeDtypeStruct((size, n), F32),
            jax.ShapeDtypeStruct((size, n), F32),
            jax.ShapeDtypeStruct((1, size, n), F32),
            jax.ShapeDtypeStruct((size, m), F32),
        ),
        in_specs=[any_space, any_space, vmem, vmem, vmem, any_space, any_space, any_space, any_space],
        out_specs=[any_space] * 4,
        scratch_shapes=scratch,
        compiler_params=pltpu.CompilerParams(
            collective_id=0, has_side_effects=True, vmem_limit_bytes=40 * 1024 * 1024),
        name="admm",
    )(design, projector, targets.reshape(1, m), sparsity.reshape(1, size), ridge_weight.reshape(1, size),
      coefficients, block_duals, row_duals, block_fits)


def solution(mesh):
    return jax.shard_map(
        per_device,
        mesh=mesh,
        in_specs=(
            P("row", "col"),
            P("col", "row", None),
            P("row"),
            P(),
            P(),
            P(None, "col"),
            P("row", None, "col"),
            P(None, "row"),
            P("col", None, "row"),
        ),
        out_specs=(P(None, "col"), P(None, "col"), P("row", None, "col"), P(None, "row")),
        check_vma=False,
    )
```

```python
import functools

import jax
import jax.numpy as jnp
from jax import lax
from jax.experimental import pallas as pl
from jax.experimental.pallas import tpu as pltpu
from jax.sharding import PartitionSpec as P

ITERS = 5
MESH = pl.DeviceIdType.MESH
BF16 = jnp.bfloat16
F32 = jnp.float32


def shrink(values, threshold):
    return jnp.maximum(values - threshold, 0.0) - jnp.maximum(-values - threshold, 0.0)


def times(left, right):
    return jnp.dot(left, right, preferred_element_type=F32)


def times_transpose(left, right):
    return lax.dot_general(left, right, (((1,), (1,)), ((), ())), preferred_element_type=F32)


def kernel(
    rows, cols, split,
    design, projector, targets, sparsity, ridge, coefficients, block_duals, row_duals, block_fits,
    o_z, o_xc, o_xd, o_yd,
    A, K, S, XD, PX, AV, XB, PY, FIT, YD, YR, U, THR, SHR, XC, HC, R, Q,
    load_a, load_k, load_v, load_x, load_z, store,
    r_send, r_recv, q_send, q_recv, a_send, a_recv, b_send, b_recv, p_send, p_recv,
):
    blocks, size, width = S.shape
    part = size // split
    me_row, me_col = lax.axis_index("row"), lax.axis_index("col")

    def partner(k):
        other, bit = me_row, 1
        while bit < rows:
            if k & bit:
                other = other + bit * (1 - 2 * ((me_row // bit) % 2))
            bit *= 2
        return other

    def beside(k):
        return {"col": lax.rem(me_col + k, cols)}

    def block_of(p):
        return p // split

    def piece(ref, p):
        if split == 1:
            return ref.at[p]
        return ref.at[p // split, pl.ds(pl.multiple_of((p % split) * part, part), part), :]

    def remote(src, dst, send, recv, device):
        return pltpu.make_async_remote_copy(
            src_ref=src, dst_ref=dst, send_sem=send, recv_sem=recv, device_id=device, device_id_type=MESH)

    def columns(c):
        return pl.ds(c * width, width)

    near = list(range(1, rows))
    far = near[::-1]

    barrier = pltpu.get_barrier_semaphore()
    peers = [{"row": partner(k)} for k in near] + [beside(k) for k in range(1, cols)]
    for peer in peers:
        pl.semaphore_signal(barrier, inc=1, device_id=peer, device_id_type=MESH)

    load_xd = [pltpu.make_async_copy(block_duals.at[0, :, columns(c)], XD.at[c], load_x.at[c]) for c in range(blocks)]
    load_fit = pltpu.make_async_copy(block_fits.at[0], FIT, load_v.at[0])
    load_yd = pltpu.make_async_copy(row_duals, YD, load_v.at[1])
    load_zs = [pltpu.make_async_copy(coefficients.at[:, columns(c)], AV.at[c], load_z.at[c]) for c in range(blocks)]
    load_as = [pltpu.make_async_copy(design.at[:, columns(c)], A.at[c], load_a.at[c]) for c in range(blocks)]
    load_kk = pltpu.make_async_copy(projector.at[0], K, load_k.at[0])
    load_fit.start()
    load_yd.start()
    for copy in load_xd:
        copy.start()
    for c in range(blocks):
        load_as[c].start()
        load_zs[c].start()
    load_kk.start()

    eye = lax.broadcasted_iota(jnp.int32, (size, size), 0) == lax.broadcasted_iota(jnp.int32, (size, size), 1)

    def upright(ref):
        return jnp.sum(jnp.where(eye, ref[...], 0.0), axis=1, keepdims=True)

    THR[...] = jnp.broadcast_to(upright(sparsity), (size, width))
    SHR[...] = jnp.broadcast_to(1.0 / (1.0 + upright(ridge)), (size, width))

    pl.semaphore_wait(barrier, len(peers))

    def share(ref, slots, send, recv, k):
        return remote(piece(ref, partner(k)), slots.at[k - 1], send.at[k - 1], recv.at[k - 1], {"row": partner(k)})

    def spread(ref, send, recv, k):
        mine = piece(ref, me_row)
        return remote(mine, mine, send.at[k - 1], recv.at[k - 1], {"row": partner(k)})

    def take(ref, send, recv, k):
        other = piece(ref, partner(k))
        remote(other, other, send.at[k - 1], recv.at[k - 1], {"row": partner(k)}).wait_recv()

    def send_fit(slot, k):
        return remote(PY.at[slot, me_col], PY.at[slot, me_col], p_send.at[slot, k - 1], p_recv.at[slot, k - 1], beside(k))

    def take_fit(slot, k):
        source = lax.rem(me_col + cols - k, cols)
        remote(PY.at[slot, source], PY.at[slot, source], p_send.at[slot, k - 1], p_recv.at[slot, k - 1], beside(k)).wait_recv()

    def sum_fit(slot):
        total = PY[slot, 0]
        for j in range(1, cols):
            total = total + PY[slot, j]
        return total

    load_fit.wait()
    load_yd.wait()
    PY[2, me_col] = FIT[...]
    for k in range(1, cols):
        send_fit(2, k).start()
    for copy in load_xd:
        copy.wait()
    for k in far:
        share(XD, Q, q_send, q_recv, k).start()

    lifted = (FIT[...] + YD[...]).astype(BF16)
    total_u = None
    for c in range(blocks):
        load_as[c].wait()
        load_zs[c].wait()
        s = AV[c] - XD[c] + times(lifted, A[c])
        S[c] = s
        u = times_transpose(s.astype(BF16), A[c])
        total_u = u if total_u is None else total_u + u
    U[...] = total_u
    load_kk.wait()

    def project(slot):
        w = times(U[...].astype(BF16), K[...]).astype(BF16)
        for k in far + [0]:
            if split == 1 or k % split == split - 1:
                c = block_of(partner(k))
                PX[c] = S[c] - times(w, A[c])
            if k:
                share(PX, R, r_send, r_recv, k).start()
        block_y = None
        for c in range(blocks):
            y = times_transpose(PX[c].astype(BF16), A[c])
            block_y = y if block_y is None else block_y + y
        PY[slot, me_col] = block_y
        for k in range(1, cols):
            send_fit(slot, k).start()

    my_rows = pl.ds(pl.multiple_of((me_row % split) * part, part), part)

    def half_col():
        return shrink(piece(AV, me_row)[...] - XC[...], THR[my_rows, :]) * SHR[my_rows, :]

    def sum_shares(ref, slots, send, recv):
        total = piece(ref, me_row)[...]
        for k in near:
            share(ref, slots, send, recv, k).wait_recv()
            total = total + slots[k - 1]
        return total

    def average():
        avg = (HC[...] + sum_shares(PX, R, r_send, r_recv)) / (rows + 1)
        piece(AV, me_row)[...] = avg
        for k in far:
            spread(AV, a_send, a_recv, k).start()
        return avg

    def row_update(slot):
        half_row = 0.5 * (YR[...] - YD[...] + targets[...])
        for k in range(1, cols):
            take_fit(slot, k)
        misfit = (half_row - sum_fit(slot)) / (cols + 1)
        YR[...] = half_row - misfit
        YD[...] = YD[...] + misfit
        return misfit

    def settle(slot):
        for k in near:
            share(PX, R, r_send, r_recv, k).wait_send()
            spread(AV, a_send, a_recv, k).wait_send()
        for k in range(1, cols):
            send_fit(slot, k).wait_send()

    project(0)

    XC[...] = -sum_shares(XD, Q, q_send, q_recv)
    HC[...] = half_col()
    for k in range(1, cols):
        take_fit(2, k)
    YR[...] = sum_fit(2)
    for k in range(1, cols):
        send_fit(2, k).wait_send()
    for k in near:
        share(XD, Q, q_send, q_recv, k).wait_send()

    def step(t, carry):
        slot = lax.rem(t, 2)
        avg = average()
        XC[...] = XC[...] + HC[...] - avg
        HC[...] = half_col()
        misfit = row_update(slot)
        lifted = (PY[slot, me_col] + misfit + YD[...]).astype(BF16)
        for c in range(blocks):
            S[c] = times(lifted, A[c])
        total_u = jnp.zeros(U.shape, F32)
        for k in [0] + near:
            if k:
                take(AV, a_send, a_recv, k)
            if split == 1 or k % split == split - 1:
                c = block_of(partner(k))
                duals = XD[c] + PX[c] - AV[c]
                XD[c] = duals
                s = AV[c] - duals + S[c]
                S[c] = s
                total_u = total_u + times_transpose(s.astype(BF16), A[c])
        U[...] = total_u
        settle(slot)
        project(1 - slot)
        return carry

    lax.fori_loop(0, ITERS - 1, step, 0)

    slot = (ITERS - 1) % 2
    piece(XB, me_row)[...] = XC[...] + HC[...]
    for k in far:
        spread(XB, b_send, b_recv, k).start()
    average()
    row_update(slot)
    stores = [pltpu.make_async_copy(YD, o_yd, store.at[0, 0])]
    stores[0].start()
    for k in near:
        spread(XB, b_send, b_recv, k).wait_send()
    for k in [0] + near:
        if k:
            take(XB, b_send, b_recv, k)
            take(AV, a_send, a_recv, k)
        if split == 1 or k % split == split - 1:
            c = block_of(partner(k))
            where = pl.ds(pl.multiple_of(c * width, width), width)
            XD[c] = XD[c] + PX[c] - AV[c]
            XB[c] = XB[c] - AV[c]
            n = len(stores)
            for ref, out in ((AV, o_z), (XB, o_xc), (XD, o_xd.at[0])):
                copy = pltpu.make_async_copy(ref.at[c], out.at[:, where], store.at[n, len(stores) - n])
                copy.start()
                stores.append(copy)
    settle(slot)
    for copy in stores:
        copy.wait()


def per_device(design, projector, targets, sparsity, ridge_weight, coefficients, block_duals, row_duals, block_fits):
    rows, cols = lax.axis_size("row"), lax.axis_size("col")
    size, n = coefficients.shape
    m = design.shape[0]
    width = max(128, n // rows)
    blocks = n // width
    split = rows // blocks
    part = size // split
    any_space = pl.BlockSpec(memory_space=pl.ANY)
    vmem = pl.BlockSpec(memory_space=pltpu.VMEM)
    dma = pltpu.SemaphoreType.DMA
    wide = pltpu.VMEM((blocks, size, width), F32)
    tall = pltpu.VMEM((size, m), F32)
    own = pltpu.VMEM((part, width), F32)
    slots = pltpu.VMEM((rows - 1, part, width), F32)
    scratch = [
        pltpu.VMEM((blocks, m, width), BF16), pltpu.VMEM((m, m), BF16),
        wide, wide, wide, wide, wide,
        pltpu.VMEM((3, cols, size, m), F32), tall, tall, tall, tall,
        pltpu.VMEM((size, width), F32), pltpu.VMEM((size, width), F32), own, own,
        slots, slots,
        dma((blocks,)), dma((1,)), dma((2,)), dma((blocks,)), dma((blocks,)), dma((3 * blocks + 1, 3)),
        dma((rows - 1,)), dma((rows - 1,)), dma((rows - 1,)), dma((rows - 1,)),
        dma((rows - 1,)), dma((rows - 1,)), dma((rows - 1,)), dma((rows - 1,)),
        dma((3, cols - 1)), dma((3, cols - 1)),
    ]
    return pl.pallas_call(
        functools.partial(kernel, rows, cols, split),
        out_shape=(
            jax.ShapeDtypeStruct((size, n), F32),
            jax.ShapeDtypeStruct((size, n), F32),
            jax.ShapeDtypeStruct((1, size, n), F32),
            jax.ShapeDtypeStruct((size, m), F32),
        ),
        in_specs=[any_space, any_space, vmem, vmem, vmem, any_space, any_space, any_space, any_space],
        out_specs=[any_space] * 4,
        scratch_shapes=scratch,
        compiler_params=pltpu.CompilerParams(
            collective_id=0, has_side_effects=True, vmem_limit_bytes=60 * 1024 * 1024),
        name="admm",
    )(design, projector, targets.reshape(1, m), sparsity.reshape(1, size), ridge_weight.reshape(1, size),
      coefficients, block_duals, row_duals, block_fits)


def solution(mesh):
    return jax.shard_map(
        per_device,
        mesh=mesh,
        in_specs=(
            P("row", "col"),
            P("col", "row", None),
            P("row"),
            P(),
            P(),
            P(None, "col"),
            P("row", None, "col"),
            P(None, "row"),
            P("col", None, "row"),
        ),
        out_specs=(P(None, "col"), P(None, "col"), P("row", None, "col"), P(None, "row")),
        check_vma=False,
    )
```

```python
import functools

import jax
import jax.numpy as jnp
from jax import lax
from jax.experimental import pallas as pl
from jax.experimental.pallas import tpu as pltpu
from jax.sharding import PartitionSpec as P

ITERS = 5
MESH = pl.DeviceIdType.MESH
BF16 = jnp.bfloat16
F32 = jnp.float32


def shrink(values, threshold):
    return jnp.maximum(values - threshold, 0.0) - jnp.maximum(-values - threshold, 0.0)


def times(left, right):
    return jnp.dot(left, right, preferred_element_type=F32)


def times_transpose(left, right):
    return lax.dot_general(left, right, (((1,), (1,)), ((), ())), preferred_element_type=F32)


HALVES = 2


def kernel(
    rows, cols, split,
    design, projector, targets, sparsity, ridge, coefficients, block_duals, row_duals, block_fits,
    o_z, o_xc, o_xd, o_yd,
    A, K, S, XD, PX, AV, XB, PY, FIT, YD, YR, U, THR, SHR, XC, HC, R, Q,
    load_a, load_k, load_v, load_x, load_z, store,
    r_send, r_recv, q_send, q_recv, a_send, a_recv, b_send, b_recv, p_send, p_recv,
):
    blocks, size, width = S.shape[1:]
    part = size // split
    me_row, me_col = lax.axis_index("row"), lax.axis_index("col")
    halves = range(HALVES)

    def partner(k):
        other, bit = me_row, 1
        while bit < rows:
            if k & bit:
                other = other + bit * (1 - 2 * ((me_row // bit) % 2))
            bit *= 2
        return other

    def beside(k):
        return {"col": lax.rem(me_col + k, cols)}

    def block_of(p):
        return p // split

    def piece(ref, h, p):
        if split == 1:
            return ref.at[h, p]
        return ref.at[h, p // split, pl.ds(pl.multiple_of((p % split) * part, part), part), :]

    def remote(src, dst, send, recv, device):
        return pltpu.make_async_remote_copy(
            src_ref=src, dst_ref=dst, send_sem=send, recv_sem=recv, device_id=device, device_id_type=MESH)

    def columns(c):
        return pl.ds(c * width, width)

    def group(h):
        return pl.ds(h * size, size)

    near = list(range(1, rows))
    far = near[::-1]

    barrier = pltpu.get_barrier_semaphore()
    peers = [{"row": partner(k)} for k in near] + [beside(k) for k in range(1, cols)]
    for peer in peers:
        pl.semaphore_signal(barrier, inc=1, device_id=peer, device_id_type=MESH)

    load_fit = [pltpu.make_async_copy(block_fits.at[0, group(h), :], FIT.at[h], load_v.at[0, h]) for h in halves]
    load_yd = [pltpu.make_async_copy(row_duals.at[group(h), :], YD.at[h], load_v.at[1, h]) for h in halves]
    load_xd = [[pltpu.make_async_copy(block_duals.at[0, group(h), columns(c)], XD.at[h, c], load_x.at[h, c])
                for c in range(blocks)] for h in halves]
    load_zs = [[pltpu.make_async_copy(coefficients.at[group(h), columns(c)], AV.at[h, c], load_z.at[h, c])
                for c in range(blocks)] for h in halves]
    load_as = [pltpu.make_async_copy(design.at[:, columns(c)], A.at[c], load_a.at[c]) for c in range(blocks)]
    load_kk = pltpu.make_async_copy(projector.at[0], K, load_k.at[0])
    for h in halves:
        load_fit[h].start()
        load_yd[h].start()
        for copy in load_xd[h]:
            copy.start()
    for c in range(blocks):
        load_as[c].start()
        load_zs[0][c].start()
    load_kk.start()
    for c in range(blocks):
        load_zs[1][c].start()

    eye = lax.broadcasted_iota(jnp.int32, (size, size), 0) == lax.broadcasted_iota(jnp.int32, (size, size), 1)

    def upright(ref, h):
        return jnp.sum(jnp.where(eye, ref[:, h * size:(h + 1) * size], 0.0), axis=1, keepdims=True)

    for h in halves:
        THR[h] = jnp.broadcast_to(upright(sparsity, h), (size, width))
        SHR[h] = jnp.broadcast_to(1.0 / (1.0 + upright(ridge, h)), (size, width))

    pl.semaphore_wait(barrier, len(peers))

    def share(ref, slots, send, recv, h, k):
        return remote(
            piece(ref, h, partner(k)), slots.at[h, k - 1], send.at[h, k - 1], recv.at[h, k - 1], {"row": partner(k)})

    def spread(ref, send, recv, h, k):
        mine = piece(ref, h, me_row)
        return remote(mine, mine, send.at[h, k - 1], recv.at[h, k - 1], {"row": partner(k)})

    def take(ref, send, recv, h, k):
        other = piece(ref, h, partner(k))
        remote(other, other, send.at[h, k - 1], recv.at[h, k - 1], {"row": partner(k)}).wait_recv()

    def fit_copy(slot, h, source, k):
        own = PY.at[slot, h, source]
        return remote(own, own, p_send.at[slot, h, k - 1], p_recv.at[slot, h, k - 1], beside(k))

    def send_fit(slot, h, k):
        return fit_copy(slot, h, me_col, k)

    def sum_fit(slot, h):
        for k in range(1, cols):
            fit_copy(slot, h, lax.rem(me_col + cols - k, cols), k).wait_recv()
        total = PY[slot, h, 0]
        for j in range(1, cols):
            total = total + PY[slot, h, j]
        return total

    for h in halves:
        load_fit[h].wait()
        load_yd[h].wait()
        PY[2, h, me_col] = FIT[h]
        for k in range(1, cols):
            send_fit(2, h, k).start()
    for h in halves:
        for copy in load_xd[h]:
            copy.wait()
        for k in far:
            share(XD, Q, q_send, q_recv, h, k).start()

    def begin(h):
        lifted = (FIT[h] + YD[h]).astype(BF16)
        total_u = None
        for c in range(blocks):
            if h == 0:
                load_as[c].wait()
            load_zs[h][c].wait()
            s = AV[h, c] - XD[h, c] + times(lifted, A[c])
            S[h, c] = s
            u = times_transpose(s.astype(BF16), A[c])
            total_u = u if total_u is None else total_u + u
        U[h] = total_u
        if h == 0:
            load_kk.wait()

    def project_x(h):
        w = times(U[h].astype(BF16), K[...]).astype(BF16)
        for k in far + [0]:
            if split == 1 or k % split == split - 1:
                c = block_of(partner(k))
                PX[h, c] = S[h, c] - times(w, A[c])
            if k:
                share(PX, R, r_send, r_recv, h, k).start()

    def project_y(h, slot):
        block_y = None
        for c in range(blocks):
            y = times_transpose(PX[h, c].astype(BF16), A[c])
            block_y = y if block_y is None else block_y + y
        PY[slot, h, me_col] = block_y
        for k in range(1, cols):
            send_fit(slot, h, k).start()

    my_rows = pl.ds(pl.multiple_of((me_row % split) * part, part), part)

    def half_col(h):
        return shrink(piece(AV, h, me_row)[...] - XC[h], THR[h, my_rows, :]) * SHR[h, my_rows, :]

    def sum_shares(ref, slots, send, recv, h):
        total = piece(ref, h, me_row)[...]
        for k in near:
            share(ref, slots, send, recv, h, k).wait_recv()
            total = total + slots[h, k - 1]
        return total

    def average(h):
        avg = (HC[h] + sum_shares(PX, R, r_send, r_recv, h)) / (rows + 1)
        piece(AV, h, me_row)[...] = avg
        for k in far:
            spread(AV, a_send, a_recv, h, k).start()
        XC[h] = XC[h] + HC[h] - avg
        HC[h] = half_col(h)

    def row_update(h, slot):
        half_row = 0.5 * (YR[h] - YD[h] + targets[...])
        misfit = (half_row - sum_fit(slot, h)) / (cols + 1)
        YR[h] = half_row - misfit
        YD[h] = YD[h] + misfit
        return misfit

    def lift(h, slot):
        misfit = row_update(h, slot)
        lifted = (PY[slot, h, me_col] + misfit + YD[h]).astype(BF16)
        for c in range(blocks):
            S[h, c] = times(lifted, A[c])

    def gather(h):
        total_u = jnp.zeros(U.shape[1:], F32)
        for k in [0] + near:
            if k:
                take(AV, a_send, a_recv, h, k)
            if split == 1 or k % split == split - 1:
                c = block_of(partner(k))
                duals = XD[h, c] + PX[h, c] - AV[h, c]
                XD[h, c] = duals
                s = AV[h, c] - duals + S[h, c]
                S[h, c] = s
                total_u = total_u + times_transpose(s.astype(BF16), A[c])
        U[h] = total_u

    def settle(h, slot):
        for k in near:
            share(PX, R, r_send, r_recv, h, k).wait_send()
            spread(AV, a_send, a_recv, h, k).wait_send()
        for k in range(1, cols):
            send_fit(slot, h, k).wait_send()

    for h in halves:
        begin(h)
        project_x(h)
    for h in halves:
        project_y(h, 0)

    for h in halves:
        XC[h] = -sum_shares(XD, Q, q_send, q_recv, h)
        HC[h] = half_col(h)
        YR[h] = sum_fit(2, h)
        for k in range(1, cols):
            send_fit(2, h, k).wait_send()
        for k in near:
            share(XD, Q, q_send, q_recv, h, k).wait_send()
        if h == 0:
            average(0)
    lift(0, 0)

    def step(t, carry):
        slot = lax.rem(t, 2)
        gather(0)
        settle(0, slot)
        project_x(0)
        average(1)
        project_y(0, 1 - slot)
        lift(1, slot)
        average(0)
        gather(1)
        settle(1, slot)
        project_x(1)
        project_y(1, 1 - slot)
        lift(0, 1 - slot)
        return carry

    lax.fori_loop(0, ITERS - 1, step, 0)

    slot = (ITERS - 1) % 2
    piece(XB, 0, me_row)[...] = XC[0]
    piece(XB, 1, me_row)[...] = XC[1] + HC[1]
    for h in (1, 0):
        for k in far:
            spread(XB, b_send, b_recv, h, k).start()
    average(1)
    row_update(1, slot)
    stores = [pltpu.make_async_copy(YD.at[h], o_yd.at[group(h), :], store.at[0, h]) for h in halves]
    for copy in stores:
        copy.start()
    for h in halves:
        for k in near:
            spread(XB, b_send, b_recv, h, k).wait_send()
        done = 1
        for k in [0] + near:
            if k:
                take(AV, a_send, a_recv, h, k)
                take(XB, b_send, b_recv, h, k)
            if split == 1 or k % split == split - 1:
                c = block_of(partner(k))
                where = pl.ds(pl.multiple_of(c * width, width), width)
                XD[h, c] = XD[h, c] + PX[h, c] - AV[h, c]
                if h == 1:
                    XB[h, c] = XB[h, c] - AV[h, c]
                for ref, out in ((AV, o_z), (XB, o_xc), (XD, o_xd.at[0])):
                    copy = pltpu.make_async_copy(ref.at[h, c], out.at[group(h), where], store.at[done, h])
                    copy.start()
                    stores.append(copy)
                    done += 1
    for h in halves:
        settle(h, slot)
    for copy in stores:
        copy.wait()


def hand_over(*refs):
    count = len(refs) // 2
    sems = refs[-1]
    copies = [pltpu.make_async_copy(refs[i], refs[count + i], sems.at[i]) for i in range(count)]
    for copy in copies:
        copy.start()
    for copy in copies:
        copy.wait()


def per_device(design, projector, targets, sparsity, ridge_weight, coefficients, block_duals, row_duals, block_fits):
    rows, cols = lax.axis_size("row"), lax.axis_size("col")
    total, n = coefficients.shape
    m = design.shape[0]
    size = total // HALVES
    width = max(128, n // rows)
    blocks = n // width
    split = rows // blocks
    part = size // split
    any_space = pl.BlockSpec(memory_space=pl.ANY)
    vmem = pl.BlockSpec(memory_space=pltpu.VMEM)
    dma = pltpu.SemaphoreType.DMA
    wide = pltpu.VMEM((HALVES, blocks, size, width), F32)
    tall = pltpu.VMEM((HALVES, size, m), F32)
    own = pltpu.VMEM((HALVES, part, width), F32)
    full = pltpu.VMEM((HALVES, size, width), F32)
    slots = pltpu.VMEM((HALVES, rows - 1, part, width), F32)
    scratch = [
        pltpu.VMEM((blocks, m, width), BF16), pltpu.VMEM((m, m), BF16),
        wide, wide, wide, wide, wide,
        pltpu.VMEM((3, HALVES, cols, size, m), F32), tall, tall, tall, tall,
        full, full, own, own, slots, slots,
        dma((blocks,)), dma((1,)), dma((2, HALVES)), dma((HALVES, blocks)), dma((HALVES, blocks)),
        dma((3 * blocks + 1, HALVES)),
    ] + [dma((HALVES, rows - 1))] * 8 + [dma((3, HALVES, cols - 1))] * 2
    shapes = (
        jax.ShapeDtypeStruct((total, n), F32),
        jax.ShapeDtypeStruct((total, n), F32),
        jax.ShapeDtypeStruct((1, total, n), F32),
        jax.ShapeDtypeStruct((total, m), F32),
    )
    results = pl.pallas_call(
        functools.partial(kernel, rows, cols, split),
        out_shape=shapes,
        in_specs=[any_space, any_space, vmem, vmem, vmem, any_space, any_space, any_space, any_space],
        out_specs=[any_space] * 4,
        scratch_shapes=scratch,
        compiler_params=pltpu.CompilerParams(
            collective_id=0, has_side_effects=True, vmem_limit_bytes=60 * 1024 * 1024),
        name="admm",
    )(design, projector, targets.reshape(1, m), sparsity.reshape(1, total), ridge_weight.reshape(1, total),
      coefficients, block_duals, row_duals, block_fits)
    return pl.pallas_call(
        hand_over,
        out_shape=shapes,
        in_specs=[any_space] * 4,
        out_specs=[any_space] * 4,
        scratch_shapes=[dma((4,))],
        compiler_params=pltpu.CompilerParams(vmem_limit_bytes=60 * 1024 * 1024),
        name="hand_over",
    )(*results)


def solution(mesh):
    return jax.shard_map(
        per_device,
        mesh=mesh,
        in_specs=(
            P("row", "col"),
            P("col", "row", None),
            P("row"),
            P(),
            P(),
            P(None, "col"),
            P("row", None, "col"),
            P(None, "row"),
            P("col", None, "row"),
        ),
        out_specs=(P(None, "col"), P(None, "col"), P("row", None, "col"), P(None, "row")),
        check_vma=False,
    )
```

```python
import functools

import jax
import jax.numpy as jnp
from jax import lax
from jax.experimental import pallas as pl
from jax.experimental.pallas import tpu as pltpu
from jax.sharding import PartitionSpec as P

ITERS = 5
MESH = pl.DeviceIdType.MESH
BF16 = jnp.bfloat16
F32 = jnp.float32


def shrink(values, threshold):
    return jnp.maximum(values - threshold, 0.0) - jnp.maximum(-values - threshold, 0.0)


def times(left, right):
    return jnp.dot(left, right, preferred_element_type=F32)


def times_transpose(left, right):
    return lax.dot_general(left, right, (((1,), (1,)), ((), ())), preferred_element_type=F32)


HALVES = 2


def kernel(
    rows, cols, split,
    design, projector, targets, sparsity, ridge, coefficients, block_duals, row_duals, block_fits,
    o_z, o_xc, o_xd, o_yd,
    A, K, S, XD, PX, AV, XB, PY, FIT, YD, YR, U, THR, SHR, XC, HC, R, Q,
    load_a, load_k, load_v, load_x, load_z, store,
    r_send, r_recv, q_send, q_recv, a_send, a_recv, b_send, b_recv, p_send, p_recv,
):
    blocks, size, width = S.shape[1:]
    part = size // split
    me_row, me_col = lax.axis_index("row"), lax.axis_index("col")
    halves = range(HALVES)

    def partner(k):
        other, bit = me_row, 1
        while bit < rows:
            if k & bit:
                other = other + bit * (1 - 2 * ((me_row // bit) % 2))
            bit *= 2
        return other

    def beside(k):
        return {"col": lax.rem(me_col + k, cols)}

    def block_of(p):
        return p // split

    def piece(ref, h, p):
        if split == 1:
            return ref.at[h, p]
        return ref.at[h, p // split, pl.ds(pl.multiple_of((p % split) * part, part), part), :]

    def remote(src, dst, send, recv, device):
        return pltpu.make_async_remote_copy(
            src_ref=src, dst_ref=dst, send_sem=send, recv_sem=recv, device_id=device, device_id_type=MESH)

    def columns(c):
        return pl.ds(c * width, width)

    def group(h):
        return pl.ds(h * size, size)

    near = list(range(1, rows))
    far = near[::-1]

    barrier = pltpu.get_barrier_semaphore()
    peers = [{"row": partner(k)} for k in near] + [beside(k) for k in range(1, cols)]
    for peer in peers:
        pl.semaphore_signal(barrier, inc=1, device_id=peer, device_id_type=MESH)

    load_fit = [pltpu.make_async_copy(block_fits.at[0, group(h), :], FIT.at[h], load_v.at[0, h]) for h in halves]
    load_yd = [pltpu.make_async_copy(row_duals.at[group(h), :], YD.at[h], load_v.at[1, h]) for h in halves]
    load_xd = [[pltpu.make_async_copy(block_duals.at[0, group(h), columns(c)], XD.at[h, c], load_x.at[h, c])
                for c in range(blocks)] for h in halves]
    load_zs = [[pltpu.make_async_copy(coefficients.at[group(h), columns(c)], AV.at[h, c], load_z.at[h, c])
                for c in range(blocks)] for h in halves]
    load_as = [pltpu.make_async_copy(design.at[:, columns(c)], A.at[c], load_a.at[c]) for c in range(blocks)]
    load_kk = pltpu.make_async_copy(projector.at[0], K, load_k.at[0])
    for h in halves:
        load_fit[h].start()
        load_yd[h].start()
        for copy in load_xd[h]:
            copy.start()
    for c in range(blocks):
        load_as[c].start()
        load_zs[0][c].start()
    load_kk.start()
    for c in range(blocks):
        load_zs[1][c].start()

    eye = lax.broadcasted_iota(jnp.int32, (size, size), 0) == lax.broadcasted_iota(jnp.int32, (size, size), 1)

    def upright(ref, h):
        return jnp.sum(jnp.where(eye, ref[:, h * size:(h + 1) * size], 0.0), axis=1, keepdims=True)

    for h in halves:
        THR[h] = jnp.broadcast_to(upright(sparsity, h), (size, width))
        SHR[h] = jnp.broadcast_to(1.0 / (1.0 + upright(ridge, h)), (size, width))

    pl.semaphore_wait(barrier, len(peers))

    def share(ref, slots, send, recv, h, k):
        return remote(
            piece(ref, h, partner(k)), slots.at[h, k - 1], send.at[h, k - 1], recv.at[h, k - 1], {"row": partner(k)})

    def spread(ref, send, recv, h, k):
        mine = piece(ref, h, me_row)
        return remote(mine, mine, send.at[h, k - 1], recv.at[h, k - 1], {"row": partner(k)})

    def take(ref, send, recv, h, k):
        other = piece(ref, h, partner(k))
        remote(other, other, send.at[h, k - 1], recv.at[h, k - 1], {"row": partner(k)}).wait_recv()

    def fit_copy(slot, h, source, k):
        own = PY.at[slot, h, source]
        return remote(own, own, p_send.at[slot, h, k - 1], p_recv.at[slot, h, k - 1], beside(k))

    def send_fit(slot, h, k):
        return fit_copy(slot, h, me_col, k)

    def sum_fit(slot, h):
        for k in range(1, cols):
            fit_copy(slot, h, lax.rem(me_col + cols - k, cols), k).wait_recv()
        total = PY[slot, h, 0]
        for j in range(1, cols):
            total = total + PY[slot, h, j]
        return total

    for h in halves:
        load_fit[h].wait()
        load_yd[h].wait()
        PY[2, h, me_col] = FIT[h]
        for k in range(1, cols):
            send_fit(2, h, k).start()
    for h in halves:
        for copy in load_xd[h]:
            copy.wait()
        for k in far:
            share(XD, Q, q_send, q_recv, h, k).start()

    def begin(h):
        lifted = (FIT[h] + YD[h]).astype(BF16)
        total_u = None
        for c in range(blocks):
            if h == 0:
                load_as[c].wait()
            load_zs[h][c].wait()
            s = AV[h, c] - XD[h, c] + times(lifted, A[c])
            S[h, c] = s
            u = times_transpose(s.astype(BF16), A[c])
            total_u = u if total_u is None else total_u + u
        U[h] = total_u
        if h == 0:
            load_kk.wait()

    def project_x(h):
        w = times(U[h].astype(BF16), K[...]).astype(BF16)
        for k in far + [0]:
            if split == 1 or k % split == split - 1:
                c = block_of(partner(k))
                PX[h, c] = S[h, c] - times(w, A[c])
            if k:
                share(PX, R, r_send, r_recv, h, k).start()

    def project_y(h, slot):
        block_y = None
        for c in range(blocks):
            y = times_transpose(PX[h, c].astype(BF16), A[c])
            block_y = y if block_y is None else block_y + y
        PY[slot, h, me_col] = block_y
        for k in range(1, cols):
            send_fit(slot, h, k).start()

    my_rows = pl.ds(pl.multiple_of((me_row % split) * part, part), part)

    def half_col(h):
        return shrink(piece(AV, h, me_row)[...] - XC[h], THR[h, my_rows, :]) * SHR[h, my_rows, :]

    def sum_shares(ref, slots, send, recv, h):
        total = piece(ref, h, me_row)[...]
        for k in near:
            share(ref, slots, send, recv, h, k).wait_recv()
            total = total + slots[h, k - 1]
        return total

    def average(h):
        avg = (HC[h] + sum_shares(PX, R, r_send, r_recv, h)) / (rows + 1)
        piece(AV, h, me_row)[...] = avg
        for k in far:
            spread(AV, a_send, a_recv, h, k).start()
        XC[h] = XC[h] + HC[h] - avg
        HC[h] = half_col(h)

    def row_update(h, slot):
        half_row = 0.5 * (YR[h] - YD[h] + targets[...].reshape(1, -1))
        misfit = (half_row - sum_fit(slot, h)) / (cols + 1)
        YR[h] = half_row - misfit
        YD[h] = YD[h] + misfit
        return misfit

    def lift(h, slot):
        misfit = row_update(h, slot)
        lifted = (PY[slot, h, me_col] + misfit + YD[h]).astype(BF16)
        for c in range(blocks):
            S[h, c] = times(lifted, A[c])

    def gather(h):
        total_u = jnp.zeros(U.shape[1:], F32)
        for k in [0] + near:
            if k:
                take(AV, a_send, a_recv, h, k)
            if split == 1 or k % split == split - 1:
                c = block_of(partner(k))
                duals = XD[h, c] + PX[h, c] - AV[h, c]
                XD[h, c] = duals
                s = AV[h, c] - duals + S[h, c]
                S[h, c] = s
                total_u = total_u + times_transpose(s.astype(BF16), A[c])
        U[h] = total_u

    def settle(h, slot):
        for k in near:
            share(PX, R, r_send, r_recv, h, k).wait_send()
            spread(AV, a_send, a_recv, h, k).wait_send()
        for k in range(1, cols):
            send_fit(slot, h, k).wait_send()

    for h in halves:
        begin(h)
        project_x(h)
    for h in halves:
        project_y(h, 0)

    for h in halves:
        XC[h] = -sum_shares(XD, Q, q_send, q_recv, h)
        HC[h] = half_col(h)
        YR[h] = sum_fit(2, h)
        for k in range(1, cols):
            send_fit(2, h, k).wait_send()
        for k in near:
            share(XD, Q, q_send, q_recv, h, k).wait_send()
        if h == 0:
            average(0)
    lift(0, 0)

    def step(t, carry):
        slot = lax.rem(t, 2)
        gather(0)
        settle(0, slot)
        project_x(0)
        average(1)
        project_y(0, 1 - slot)
        lift(1, slot)
        average(0)
        gather(1)
        settle(1, slot)
        project_x(1)
        project_y(1, 1 - slot)
        lift(0, 1 - slot)
        return carry

    lax.fori_loop(0, ITERS - 1, step, 0)

    slot = (ITERS - 1) % 2
    piece(XB, 0, me_row)[...] = XC[0]
    piece(XB, 1, me_row)[...] = XC[1] + HC[1]
    for h in (1, 0):
        for k in far:
            spread(XB, b_send, b_recv, h, k).start()
    average(1)
    row_update(1, slot)
    stores = [pltpu.make_async_copy(YD.at[h], o_yd.at[group(h), :], store.at[0, h]) for h in halves]
    for copy in stores:
        copy.start()
    for h in halves:
        for k in near:
            spread(XB, b_send, b_recv, h, k).wait_send()
        done = 1
        for k in [0] + near:
            if k:
                take(AV, a_send, a_recv, h, k)
                take(XB, b_send, b_recv, h, k)
            if split == 1 or k % split == split - 1:
                c = block_of(partner(k))
                where = pl.ds(pl.multiple_of(c * width, width), width)
                XD[h, c] = XD[h, c] + PX[h, c] - AV[h, c]
                if h == 1:
                    XB[h, c] = XB[h, c] - AV[h, c]
                for ref, out in ((AV, o_z), (XB, o_xc), (XD, o_xd.at[0])):
                    copy = pltpu.make_async_copy(ref.at[h, c], out.at[group(h), where], store.at[done, h])
                    copy.start()
                    stores.append(copy)
                    done += 1
    for h in halves:
        settle(h, slot)
    for copy in stores:
        copy.wait()


def per_device(design, projector, targets, sparsity, ridge_weight, coefficients, block_duals, row_duals, block_fits):
    rows, cols = lax.axis_size("row"), lax.axis_size("col")
    total, n = coefficients.shape
    m = design.shape[0]
    size = total // HALVES
    width = max(128, n // rows)
    blocks = n // width
    split = rows // blocks
    part = size // split
    any_space = pl.BlockSpec(memory_space=pl.ANY)
    hbm = pl.BlockSpec(memory_space=pltpu.HBM)
    vmem = pl.BlockSpec(memory_space=pltpu.VMEM)
    dma = pltpu.SemaphoreType.DMA
    wide = pltpu.VMEM((HALVES, blocks, size, width), F32)
    tall = pltpu.VMEM((HALVES, size, m), F32)
    own = pltpu.VMEM((HALVES, part, width), F32)
    full = pltpu.VMEM((HALVES, size, width), F32)
    slots = pltpu.VMEM((HALVES, rows - 1, part, width), F32)
    scratch = [
        pltpu.VMEM((blocks, m, width), BF16), pltpu.VMEM((m, m), BF16),
        wide, wide, wide, wide, wide,
        pltpu.VMEM((3, HALVES, cols, size, m), F32), tall, tall, tall, tall,
        full, full, own, own, slots, slots,
        dma((blocks,)), dma((1,)), dma((2, HALVES)), dma((HALVES, blocks)), dma((HALVES, blocks)),
        dma((3 * blocks + 1, HALVES)),
    ] + [dma((HALVES, rows - 1))] * 8 + [dma((3, HALVES, cols - 1))] * 2
    shapes = (
        pltpu.VMEM((total, n), F32),
        pltpu.VMEM((total, n), F32),
        pltpu.VMEM((1, total, n), F32),
        pltpu.VMEM((total, m), F32),
    )
    return pl.pallas_call(
        functools.partial(kernel, rows, cols, split),
        out_shape=shapes,
        in_specs=[hbm, hbm, vmem, vmem, vmem, hbm, hbm, hbm, hbm],
        out_specs=[vmem] * 4,
        scratch_shapes=scratch,
        compiler_params=pltpu.CompilerParams(
            collective_id=0, has_side_effects=True, vmem_limit_bytes=59 * 1024 * 1024),
        name="admm",
    )(design, projector, targets, sparsity.reshape(1, total), ridge_weight.reshape(1, total),
      coefficients, block_duals, row_duals, block_fits)


def solution(mesh):
    return jax.shard_map(
        per_device,
        mesh=mesh,
        in_specs=(
            P("row", "col"),
            P("col", "row", None),
            P("row"),
            P(),
            P(),
            P(None, "col"),
            P("row", None, "col"),
            P(None, "row"),
            P("col", None, "row"),
        ),
        out_specs=(P(None, "col"), P(None, "col"), P("row", None, "col"), P(None, "row")),
        check_vma=False,
    )
```
